32 devices in a mesh: dp: 4 (over y, x), expert: 4 (over z), tensor: 2 (over core).
Axes of the slice: x: 2, y: 2, z: 4, core: 2. Of those that a mesh axis runs over, the one named last changes fastest.
Arguments:
- tokens: bfloat16 [448, 4096], P(('dp', 'expert'), 'tensor'), may hold values from -6 to 6
- route_ids: int32 [448, 2], P(('dp', 'expert')), may hold values from 0 to 3, all different within a row; in each aligned block of 28 rows (0 to 27, 28 to 55, ...) at most 17 rows name the same one
- route_gates: float32 [448, 2], P(('dp', 'expert')), may hold values from 0.2 to 1
- d_out: bfloat16 [448, 4096], P(('dp', 'expert'), 'tensor'), may hold values from -6 to 6
- gate_saved: bfloat16 [4, 4096, 8192], P(None, 'tensor', ('dp', 'expert')), may hold values from -0.09375 to 0.09375
- up_saved: bfloat16 [4, 4096, 8192], P(None, 'tensor', ('dp', 'expert')), may hold values from -0.09375 to 0.09375
- down_saved: bfloat16 [4, 4096, 8192], P(None, 'tensor', ('dp', 'expert')), may hold values from -0.0625 to 0.0625
Outputs:
- out: bfloat16 [448, 4096], P(('dp', 'expert'), 'tensor')
- d_tokens: bfloat16 [448, 4096], P(('dp', 'expert'), 'tensor')
- grad_gate: bfloat16 [4, 4096, 8192], P('expert', 'tensor', 'dp')
- grad_up: bfloat16 [4, 4096, 8192], P('expert', 'tensor', 'dp')
- grad_down: bfloat16 [4, 4096, 8192], P('expert', 'tensor', 'dp')
The draws below stay inside these ranges and needn't reach their ends.
Inputs may be any that keep to these rules, and one draw needn't show every extreme that they name: `route_ids`: each token names two different experts. Among the 28 tokens of one aligned block of the token dimension no expert is named more than 17 times, and in some block one expert is named exactly 17 times.
All inputs are finite; a program needn't handle non-finite values.
Results may differ from the reference program's by a relative error of at most 0.028.
Values may be sent and summed in bfloat16 or wider, within the bound.
A program may use at most 128 MiB of HBM per device.

```python
import math
import jax
import jax.numpy as jnp
import numpy as np
from jax import lax

D = 4096
FF = 8192
TOK_DEV = 28
EXPERTS = 4
CAP = 17
TOKENS = 448
ROWS = 272
N_DP = 4
N_EXPERT = 4
N_TENSOR = 2


def block_levels(key, dims, shards, low, high):
    loudness = 1.0
    for position, blocks in shards:
        draws = jax.random.uniform(jax.random.fold_in(jax.random.fold_in(key, 6), position), (blocks,), jnp.float32, low / len(shards), high / len(shards))
        loudness = loudness * jnp.repeat(jnp.exp(draws), dims[position] // blocks).reshape((-1,) + (1,) * (len(dims) - 1 - position))
    return loudness


def routed_block(stream_key, own, number, rows, count, top, reach, lean):
    sequence = jax.random.permutation(stream_key, count)
    heavy_load, common = load_shares(count, rows * top, reach, lean, True), load_shares(count, rows * top, reach, lean, False)
    places = jnp.arange(count)

    def named(sizes, rotation):
        used = int((sizes > 0).sum())
        fixed = max(1, used // 4)
        moved = fixed + (places - fixed + rotation * (used - fixed)) % max(1, count - fixed)
        return jnp.zeros((count,), jnp.int32).at[sequence[jnp.where(places < fixed, places, moved)]].set(jnp.asarray(sizes, jnp.int32))

    sizes = jnp.where(number % 4 == 0, named(heavy_load, number // 4), named(common, number - number // 4 - 1))
    mixed = jax.random.permutation(jax.random.fold_in(own, 3), count)
    giver, sink = mixed[0:count // 2 * 2:2], mixed[1:count // 2 * 2:2]
    margin = jnp.minimum(sizes[giver] - 1, reach - sizes[sink]) // 2
    margin = jnp.where((giver == sequence[0]) | (sink == sequence[0]) | (sizes[sink] == 0), 0, jnp.maximum(margin, 0))
    moved = jax.random.randint(jax.random.fold_in(own, 4), (count // 2,), 0, 1 << 20) % (margin + 1)
    sizes = sizes.at[giver].add(-moved).at[sink].add(moved)
    labels = jnp.searchsorted(jnp.cumsum(sizes), jnp.arange(rows * top), side="right").astype(jnp.int32)
    grid = labels.reshape(top, rows).T
    grid = grid[jax.random.permutation(jax.random.fold_in(own, 1), rows)]
    rotation = jax.random.randint(jax.random.fold_in(own, 2), (rows, 1), 0, top)
    return jnp.take_along_axis(grid, (jnp.arange(top)[None, :] + rotation) % top, axis=1)


def load_shares(number_of, total, reach, skew, full):
    loads = [(1 << 20) // math.isqrt(standing ** skew) + 1 for standing in range(1, number_of + 1)]
    largest = reach if full else min(reach, max(-(-total // number_of), total * loads[0] // sum(loads)))
    least = 1 if total - largest >= number_of - 1 else 0
    given, rest = [largest] + [least] * (number_of - 1), total - largest - least * (number_of - 1)
    while rest > 0:
        candidates = [i for i in range(1, number_of) if given[i] < largest] or [i for i in range(1, number_of) if given[i] < reach]
        whole, left = sum([loads[i] for i in candidates]), rest
        for i in candidates:
            more = min(reach - given[i], max(1, left * loads[i] // whole), rest)
            given[i] = given[i] + more
            rest = rest - more
    return np.array(given)


def centred(own_key, shape, scale, reach, pieces=(), kind=jnp.bfloat16):
    array = jax.random.normal(own_key, shape, jnp.float32) * scale
    if len(pieces) > 0:
        array = block_levels(own_key, shape, pieces, -0.22, 0.18) * array
    return jnp.clip(array, min=-reach, max=reach).astype(kind)


def setup_inputs(seed: int = 0) -> dict:
    keys = jax.random.split(jax.random.key(seed), 8)
    tokens = centred(keys[0], (TOKENS, D), 1.0, 6.0, ((0, 16), (1, 2)))
    route_ids_keys = jax.random.split(jax.random.fold_in(keys[1], 1), TOKENS // TOK_DEV)
    route_ids_turns = jax.random.permutation(jax.random.fold_in(keys[1], 3), TOKENS // TOK_DEV)
    route_ids = jax.vmap(lambda own, number: routed_block(jax.random.fold_in(keys[1], 2), own, number, TOK_DEV, N_EXPERT, 2, CAP, 2))(route_ids_keys, route_ids_turns).reshape((TOKENS, 2))
    route_gates = jnp.clip(0.2 + 0.8 * jax.random.uniform(keys[2], (TOKENS, 2), jnp.float32) ** block_levels(keys[2], (TOKENS, 2), ((0, 16),), -0.2, 0.2), 0.2, 1.0)
    d_out = centred(keys[3], (TOKENS, D), 1.0, 6.0, ((0, 16), (1, 2)))
    gate_saved = centred(keys[4], (EXPERTS, D, FF), D ** -0.5, 0.09375, ((1, 2), (2, 16)))
    up_saved = centred(keys[5], (EXPERTS, D, FF), D ** -0.5, 0.09375, ((1, 2), (2, 16)))
    down_saved = centred(keys[6], (EXPERTS, D, FF), FF ** -0.5, 0.0625, ((1, 2), (2, 16)))
    return dict(tokens=tokens, route_ids=route_ids, route_gates=route_gates, d_out=d_out, gate_saved=gate_saved, up_saved=up_saved, down_saved=down_saved)


def swiglu_pair(gate_sum, up_sum, back_sum):
    sigmoid_gate = jax.nn.sigmoid(gate_sum)
    silu_gate = gate_sum * sigmoid_gate
    hidden = (silu_gate * up_sum).astype(jnp.bfloat16)
    d_up = (back_sum * silu_gate).astype(jnp.bfloat16)
    d_gate = (back_sum * up_sum * sigmoid_gate * (1.0 + gate_sum * (1.0 - sigmoid_gate))).astype(jnp.bfloat16)
    return hidden, d_gate, d_up


def block_sum(rows_in, weight):
    width_part = D // N_TENSOR
    running = jnp.zeros((rows_in.shape[0], weight.shape[1]), jnp.float32)
    for block_index in range(N_TENSOR):
        lower = block_index * width_part
        upper = lower + width_part
        partial_product = jnp.dot(rows_in[:, lower:upper], weight[lower:upper], preferred_element_type=jnp.float32)
        rounded = lax.optimization_barrier(partial_product.astype(jnp.bfloat16))
        running = running + rounded.astype(jnp.float32)
    return running


def contract_rows(left_side, right_side):
    return lax.dot_general(left_side, right_side, (((0,), (0,)), ((), ())), preferred_element_type=jnp.float32)


def contract_last(left_side, right_side):
    return lax.dot_general(left_side, right_side, (((1,), (1,)), ((), ())), preferred_element_type=jnp.float32)


def hidden_block_sum(pairs):
    hidden_part = FF // N_DP
    running = jnp.zeros((pairs[0][0].shape[0], pairs[0][1].shape[0]), jnp.float32)
    for block_index in range(N_DP):
        lower = block_index * hidden_part
        upper = lower + hidden_part
        partial_product = jnp.zeros_like(running)
        for left_side, right_side in pairs:
            partial_product = partial_product + contract_last(left_side[:, lower:upper], right_side[:, lower:upper])
        rounded = lax.optimization_barrier(partial_product.astype(jnp.bfloat16))
        running = running + rounded.astype(jnp.float32)
    return running


def expert_pass(operands):
    rows_x, rows_dy, w_gate, w_up, w_down = operands
    gate_sum = block_sum(rows_x, w_gate)
    up_sum = block_sum(rows_x, w_up)
    back_sum = block_sum(rows_dy, w_down)
    hidden, d_gate, d_up = swiglu_pair(gate_sum, up_sum, back_sum)
    expert_out = hidden_block_sum(((hidden, w_down),)).astype(jnp.bfloat16)
    expert_dx = hidden_block_sum(((d_gate, w_gate), (d_up, w_up))).astype(jnp.bfloat16)
    grad_gate = contract_rows(rows_x, d_gate).astype(jnp.bfloat16)
    grad_up = contract_rows(rows_x, d_up).astype(jnp.bfloat16)
    grad_down = contract_rows(rows_dy, hidden).astype(jnp.bfloat16)
    return expert_out, expert_dx, grad_gate, grad_up, grad_down


def reference(tokens, route_ids, route_gates, d_out, gate_saved, up_saved, down_saved):
    blocks = TOKENS // TOK_DEV
    block_ids = route_ids.reshape(blocks, TOK_DEV, 2)
    onehot = (block_ids[..., None] == jnp.arange(EXPERTS, dtype=jnp.int32)).astype(jnp.int32)
    flat_hits = onehot.reshape(blocks, TOK_DEV * 2, EXPERTS)
    before = (jnp.cumsum(flat_hits, axis=1) - flat_hits).astype(jnp.int32)
    slot_index = jnp.sum(before * flat_hits, axis=2).astype(jnp.int32).reshape(blocks, TOK_DEV, 2)
    row_index = (jnp.arange(blocks, dtype=jnp.int32)[:, None, None] * CAP + slot_index).astype(jnp.int32)
    token_blocks = tokens.reshape(blocks, TOK_DEV, 1, D)
    token_copies = jnp.broadcast_to(token_blocks, (blocks, TOK_DEV, 2, D))
    gates = route_gates.reshape(blocks, TOK_DEV, 2, 1)
    gated_dy = (gates * d_out.reshape(blocks, TOK_DEV, 1, D).astype(jnp.float32)).astype(jnp.bfloat16)
    rows_x = jnp.zeros((EXPERTS, ROWS, D), jnp.bfloat16).at[block_ids, row_index].set(token_copies)
    rows_dy = jnp.zeros((EXPERTS, ROWS, D), jnp.bfloat16).at[block_ids, row_index].set(gated_dy)
    expert_out, expert_dx, grad_gate, grad_up, grad_down = lax.map(
        expert_pass, (rows_x, rows_dy, gate_saved, up_saved, down_saved))
    picked_out = expert_out[block_ids, row_index].astype(jnp.float32)
    picked_dx = expert_dx[block_ids, row_index].astype(jnp.float32)
    out = jnp.sum(gates * picked_out, axis=2).reshape(TOKENS, D).astype(jnp.bfloat16)
    d_tokens = jnp.sum(picked_dx, axis=2).reshape(TOKENS, D).astype(jnp.bfloat16)
    return out, d_tokens, grad_gate, grad_up, grad_down
```

```python
import jax
import jax.numpy as jnp
from jax import lax
from jax.sharding import PartitionSpec as P

BLOCKS = ("dp", "expert")
F32 = jnp.float32
BF16 = jnp.bfloat16


def swiglu_pair(gate_sum, up_sum, back_sum):
    sigmoid_gate = jax.nn.sigmoid(gate_sum)
    silu_gate = gate_sum * sigmoid_gate
    hidden = (silu_gate * up_sum).astype(BF16)
    d_up = (back_sum * silu_gate).astype(BF16)
    d_gate = (back_sum * up_sum * sigmoid_gate * (1.0 + gate_sum * (1.0 - sigmoid_gate))).astype(BF16)
    return (hidden, d_gate, d_up)


def contract_rows(left_side, right_side):
    return lax.dot_general(
        left_side, right_side, (((0,), (0,)), ((), ())), preferred_element_type=F32
    )


def feature_sum(part):
    if lax.axis_size("tensor") == 2:
        other = lax.ppermute(part, "tensor", [(0, 1), (1, 0)])
        return part.astype(F32) + other.astype(F32)
    return lax.psum(part, "tensor").astype(F32)


def join_lanes(piece):
    count = lax.axis_size("tensor")
    if count == 2:
        other = lax.ppermute(piece, "tensor", [(0, 1), (1, 0)])
        first = lax.axis_index("tensor") == 0
        return jnp.concatenate(
            [jnp.where(first, piece, other), jnp.where(first, other, piece)], axis=-1
        )
    return lax.all_gather(piece, "tensor", axis=piece.ndim - 1, tiled=True)


def local(tokens, route_ids, route_gates, d_out, gate_saved, up_saved, down_saved):
    experts = lax.axis_size("expert")
    blocks = lax.axis_size("dp") * experts
    tok_count, width = tokens.shape
    capacity = 5 * tok_count // 8
    rows = blocks * capacity
    hidden_width = gate_saved.shape[2]
    block = lax.axis_index("dp") * experts + lax.axis_index("expert")

    flat_ids = route_ids.reshape(-1)
    order = jnp.arange(2 * tok_count, dtype=jnp.int32)
    earlier = (flat_ids[None, :] == flat_ids[:, None]) & (order[None, :] < order[:, None])
    slot = jnp.sum(earlier.astype(jnp.int32), axis=1).reshape(tok_count, 2)
    target = route_ids * rows + block * capacity + slot
    routes = jnp.concatenate([target.astype(F32), route_gates], axis=1)
    routes = lax.all_gather(routes, BLOCKS, axis=0, tiled=False).reshape(-1, 4)
    all_tokens = lax.all_gather(tokens, BLOCKS, axis=0, tiled=False).reshape(-1, width)
    all_d_out = lax.all_gather(d_out, BLOCKS, axis=0, tiled=False).reshape(-1, width)

    targets = routes[:, :2].astype(jnp.int32).T
    gates = routes[:, 2:].T
    places = jnp.arange(experts * rows, dtype=jnp.int32)[:, None]
    first, second = places == targets[0][None], places == targets[1][None]
    placer = (first | second).astype(BF16)
    row_gates = jnp.sum(
        jnp.where(first, gates[0][None], 0.0) + jnp.where(second, gates[1][None], 0.0),
        axis=1, keepdims=True,
    )
    rows_x = jnp.dot(placer, all_tokens, preferred_element_type=F32)
    rows_x = rows_x.astype(BF16).reshape(experts, rows, width)
    rows_dy = jnp.dot(placer, all_d_out, preferred_element_type=F32) * row_gates
    rows_dy = rows_dy.astype(BF16).reshape(experts, rows, width)

    def forward(left, right):
        return jnp.einsum("erd,edf->erf", left, right, preferred_element_type=F32).astype(BF16)

    def backward(left, right):
        return jnp.einsum("erf,edf->erd", left, right, preferred_element_type=F32)

    gate_sum = feature_sum(forward(rows_x, gate_saved))
    up_sum = feature_sum(forward(rows_x, up_saved))
    back_sum = feature_sum(forward(rows_dy, down_saved))
    hidden, d_gate, d_up = swiglu_pair(gate_sum, up_sum, back_sum)

    share = hidden_width // lax.axis_size("tensor")
    start = lax.axis_index("tensor") * share

    def to_owner(array):
        piece = lax.dynamic_slice_in_dim(array, start, share, axis=2)
        piece = lax.all_to_all(piece, "expert", split_axis=0, concat_axis=0, tiled=True)
        piece = join_lanes(piece)
        return piece.transpose(1, 0, 2).reshape(rows, experts * hidden_width)

    own_hidden, own_d_gate, own_d_up = to_owner(hidden), to_owner(d_gate), to_owner(d_up)

    def to_tokens(slot_rows):
        sums = contract_rows(placer, slot_rows.reshape(experts * rows, width).astype(BF16))
        sums = sums.astype(BF16).reshape(blocks, tok_count, width)
        return lax.psum_scatter(sums, BLOCKS, scatter_dimension=0, tiled=False)

    out = to_tokens(backward(hidden, down_saved) * row_gates.reshape(experts, rows, 1))
    d_tokens = to_tokens(backward(d_gate, gate_saved) + backward(d_up, up_saved))

    mine = lax.axis_index("expert")
    own_x = lax.dynamic_index_in_dim(rows_x, mine, 0, keepdims=False)
    own_dy = lax.dynamic_index_in_dim(rows_dy, mine, 0, keepdims=False)
    grad_gate = contract_rows(own_x, own_d_gate).astype(BF16)[None]
    grad_up = contract_rows(own_x, own_d_up).astype(BF16)[None]
    grad_down = contract_rows(own_dy, own_hidden).astype(BF16)[None]
    return (out, d_tokens, grad_gate, grad_up, grad_down)


def solution(mesh):
    in_specs = (
        P(BLOCKS, "tensor"),
        P(BLOCKS, None),
        P(BLOCKS, None),
        P(BLOCKS, "tensor"),
        P(None, "tensor", BLOCKS),
        P(None, "tensor", BLOCKS),
        P(None, "tensor", BLOCKS),
    )
    out_specs = (
        P(BLOCKS, "tensor"),
        P(BLOCKS, "tensor"),
        P("expert", "tensor", "dp"),
        P("expert", "tensor", "dp"),
        P("expert", "tensor", "dp"),
    )
    return jax.shard_map(local, mesh=mesh, in_specs=in_specs, out_specs=out_specs, check_vma=False)
```

```python
import jax
import jax.numpy as jnp
from jax import lax
from jax.sharding import PartitionSpec as P

BLOCKS = ("dp", "expert")
F32 = jnp.float32
BF16 = jnp.bfloat16


def swiglu_pair(gate_sum, up_sum, back_sum):
    sigmoid_gate = jax.nn.sigmoid(gate_sum)
    silu_gate = gate_sum * sigmoid_gate
    hidden = (silu_gate * up_sum).astype(BF16)
    d_up = (back_sum * silu_gate).astype(BF16)
    d_gate = (back_sum * up_sum * sigmoid_gate * (1.0 + gate_sum * (1.0 - sigmoid_gate))).astype(BF16)
    return (hidden, d_gate, d_up)


def contract_rows(left_side, right_side):
    return lax.dot_general(
        left_side, right_side, (((0,), (0,)), ((), ())), preferred_element_type=F32
    )


def feature_sum(part):
    if lax.axis_size("tensor") == 2:
        other = lax.ppermute(part, "tensor", [(0, 1), (1, 0)])
        return part.astype(F32) + other.astype(F32)
    return lax.psum(part, "tensor").astype(F32)


def join_lanes(piece):
    count = lax.axis_size("tensor")
    if count == 2:
        other = lax.ppermute(piece, "tensor", [(0, 1), (1, 0)])
        first = lax.axis_index("tensor") == 0
        return jnp.concatenate(
            [jnp.where(first, piece, other), jnp.where(first, other, piece)], axis=-1
        )
    return lax.all_gather(piece, "tensor", axis=piece.ndim - 1, tiled=True)


def spread(block, axes):
    copies = jnp.broadcast_to(block[None], (lax.axis_size(axes),) + block.shape)
    return lax.all_to_all(copies, axes, split_axis=0, concat_axis=0, tiled=True)


def collect(sums, axis):
    parts = lax.all_to_all(sums, axis, split_axis=0, concat_axis=0, tiled=True)
    return jnp.sum(parts.astype(F32), axis=0).astype(BF16)


def local(tokens, route_ids, route_gates, d_out, gate_saved, up_saved, down_saved):
    experts = lax.axis_size("expert")
    blocks = lax.axis_size("dp") * experts
    tok_count, width = tokens.shape
    capacity = 5 * tok_count // 8
    rows = blocks * capacity
    hidden_width = gate_saved.shape[2]
    block = lax.axis_index("dp") * experts + lax.axis_index("expert")

    flat_ids = route_ids.reshape(-1)
    order = jnp.arange(2 * tok_count, dtype=jnp.int32)
    earlier = (flat_ids[None, :] == flat_ids[:, None]) & (order[None, :] < order[:, None])
    slot = jnp.sum(earlier.astype(jnp.int32), axis=1).reshape(tok_count, 2)
    target = route_ids * rows + block * capacity + slot
    routes = jnp.concatenate([target.astype(F32), route_gates], axis=1)
    padding = -tok_count % 16
    padded = tok_count + padding
    routes = jnp.pad(routes, ((0, padding), (0, 0)), constant_values=-1.0)
    routes = spread(routes, BLOCKS).reshape(-1, 4)

    def gather(own):
        own = jnp.pad(own, ((0, padding), (0, 0)))
        return spread(spread(own, "expert"), "dp").reshape(-1, width)

    all_tokens = gather(tokens)
    all_d_out = gather(d_out)

    targets = routes[:, :2].astype(jnp.int32).T
    gates = routes[:, 2:].T
    places = jnp.arange(experts * rows, dtype=jnp.int32)[:, None]
    first, second = places == targets[0][None], places == targets[1][None]
    placer = (first | second).astype(BF16)
    row_gates = jnp.sum(
        jnp.where(first, gates[0][None], 0.0) + jnp.where(second, gates[1][None], 0.0),
        axis=1, keepdims=True,
    )
    rows_x = jnp.dot(placer, all_tokens, preferred_element_type=F32)
    rows_x = rows_x.astype(BF16).reshape(experts, rows, width)
    rows_dy = jnp.dot(placer, all_d_out, preferred_element_type=F32) * row_gates
    rows_dy = rows_dy.astype(BF16).reshape(experts, rows, width)

    def forward(left, right):
        return jnp.einsum("erd,edf->erf", left, right, preferred_element_type=F32).astype(BF16)

    def backward(left, right):
        return jnp.einsum("erf,edf->erd", left, right, preferred_element_type=F32)

    gate_sum = feature_sum(forward(rows_x, gate_saved))
    up_sum = feature_sum(forward(rows_x, up_saved))
    back_sum = feature_sum(forward(rows_dy, down_saved))
    hidden, d_gate, d_up = swiglu_pair(gate_sum, up_sum, back_sum)

    share = hidden_width // lax.axis_size("tensor")
    start = lax.axis_index("tensor") * share

    def to_owner(array):
        piece = lax.dynamic_slice_in_dim(array, start, share, axis=2)
        piece = lax.all_to_all(piece, "expert", split_axis=0, concat_axis=0, tiled=True)
        piece = join_lanes(piece)
        return piece.transpose(1, 0, 2).reshape(rows, experts * hidden_width)

    own_hidden, own_d_gate, own_d_up = to_owner(hidden), to_owner(d_gate), to_owner(d_up)

    def to_tokens(slot_rows):
        sums = contract_rows(placer, slot_rows.reshape(experts * rows, width).astype(BF16))
        sums = sums.astype(BF16).reshape(-1, experts, padded, width)
        return collect(collect(sums, "dp"), "expert")[:tok_count]

    out = to_tokens(backward(hidden, down_saved) * row_gates.reshape(experts, rows, 1))
    d_tokens = to_tokens(backward(d_gate, gate_saved) + backward(d_up, up_saved))

    mine = lax.axis_index("expert")
    own_x = lax.dynamic_index_in_dim(rows_x, mine, 0, keepdims=False)
    own_dy = lax.dynamic_index_in_dim(rows_dy, mine, 0, keepdims=False)
    grad_gate = contract_rows(own_x, own_d_gate).astype(BF16)[None]
    grad_up = contract_rows(own_x, own_d_up).astype(BF16)[None]
    grad_down = contract_rows(own_dy, own_hidden).astype(BF16)[None]
    return (out, d_tokens, grad_gate, grad_up, grad_down)


def solution(mesh):
    in_specs = (
        P(BLOCKS, "tensor"),
        P(BLOCKS, None),
        P(BLOCKS, None),
        P(BLOCKS, "tensor"),
        P(None, "tensor", BLOCKS),
        P(None, "tensor", BLOCKS),
        P(None, "tensor", BLOCKS),
    )
    out_specs = (
        P(BLOCKS, "tensor"),
        P(BLOCKS, "tensor"),
        P("expert", "tensor", "dp"),
        P("expert", "tensor", "dp"),
        P("expert", "tensor", "dp"),
    )
    return jax.shard_map(local, mesh=mesh, in_specs=in_specs, out_specs=out_specs, check_vma=False)
```
